32 devices in a mesh: section: 2 (over core), seq: 2 (over x), head: 8 (over z, y).
Axes of the slice: x: 2, y: 2, z: 4, core: 2. Of those that a mesh axis runs over, the one named last changes fastest.
Arguments:
- hidden: bfloat16 [2, 512, 4096], P('section', 'seq', 'head'), may hold values from -6 to 6
- gain: bfloat16 [2, 4096], P('section'), may hold values from 0.5 to 1.5
- w_query: bfloat16 [2, 4096, 2048], P('section', None, 'head'), may hold values from -0.0234375 to 0.0234375
- w_key: bfloat16 [2, 4096, 2048], P('section', None, 'head'), may hold values from -0.09375 to 0.09375
- w_value: bfloat16 [2, 4096, 2048], P('section', None, 'head'), may hold values from -0.09375 to 0.09375
- w_out: bfloat16 [2, 2048, 4096], P('section', 'head'), may hold values from -0.5 to 0.5
- memory: bfloat16 [384, 4096], P(('section', 'seq', 'head')), may hold values from -6 to 6
- keep: int32 [384], P(('section', 'seq', 'head')), may hold values 0 or 1
Outputs:
- next_inputs: bfloat16 [2, 512, 4096], P('section', 'seq', 'head')
The draws below stay inside these ranges and needn't reach their ends.
All inputs are finite; a program needn't handle non-finite values. No bound on the sum of `keep` on one device may be relied on, other than what follows from the above.
Results may differ from the reference program's by a relative error of at most 0.014.
Values may be sent and summed in bfloat16 or wider, within the bound.
A program may use at most 64 MiB of HBM per device.

```python
import jax
import jax.numpy as jnp
from jax import lax

D = 4096
HEADS = 32
HEAD_DIM = 64
SECTIONS = 2
QTOK = 512
MTOK = 384


def set_ends(drawn, stream_key, low, largest):
    dims = drawn.shape
    spot = [jax.random.randint(jax.random.fold_in(stream_key, axis), (), 0, dims[axis]) for axis in range(len(dims))]
    drawn = drawn.at[tuple(spot)].set(low)
    longest = dims.index(max(dims))
    spot[longest] = (spot[longest] + 1) % dims[longest]
    return drawn.at[tuple(spot)].set(largest)


def level_of(own_key, shape, pieces, low, largest):
    loudness, own = 1.0, jax.random.fold_in(own_key, 6)
    for position, parts in pieces:
        steps = jnp.exp(jax.random.uniform(jax.random.fold_in(own, position), (parts,), jnp.float32, low / len(pieces), largest / len(pieces)))
        loudness = loudness * jnp.repeat(steps, shape[position] // parts).reshape([-1 if axis == position else 1 for axis in range(len(shape))])
    return loudness


def scatter_about(own_key, extent, scale, reach, pieces=(), held_as=jnp.bfloat16):
    drawn = jax.random.normal(own_key, extent, jnp.float32) * scale
    if len(pieces) > 0:
        drawn = level_of(own_key, extent, pieces, -0.22, 0.18) * drawn
    return jnp.clip(drawn, min=-reach, max=reach).astype(held_as)


def setup_inputs(seed: int = 0) -> dict:
    keys = jax.random.split(jax.random.key(seed), 9)
    hidden = scatter_about(keys[0], (SECTIONS, QTOK, D), 1.0, 6.0, ((0, 2), (1, 2), (2, 8)))
    gain = jnp.clip(1.0 + 0.1 * jax.random.normal(keys[1], (SECTIONS, D), jnp.float32), 0.5, 1.5).astype(jnp.bfloat16)
    w_query = scatter_about(keys[2], (SECTIONS, D, HEADS * HEAD_DIM), (16 * D) ** -0.5, 0.0234375, ((0, 2), (2, 8)))
    w_key = scatter_about(keys[3], (SECTIONS, D, HEADS * HEAD_DIM), D ** -0.5, 0.09375, ((0, 2), (2, 8)))
    w_value = scatter_about(keys[4], (SECTIONS, D, HEADS * HEAD_DIM), D ** -0.5, 0.09375, ((0, 2), (2, 8)))
    w_out = scatter_about(keys[5], (SECTIONS, HEADS * HEAD_DIM, D), 128 ** -0.5, 0.5, ((0, 2), (1, 8)))
    memory = scatter_about(keys[6], (MTOK, D), 1.0, 6.0, ((0, 32),))
    keep = set_ends((jax.random.randint(keys[7], (MTOK,), 0, 8) < 7).astype(jnp.int32), jax.random.fold_in(keys[7], 1), 0, 1)
    return dict(hidden=hidden, gain=gain, w_query=w_query, w_key=w_key, w_value=w_value, w_out=w_out, memory=memory, keep=keep)


def section_update(items, memory, mask_bias):
    features, gain_row, query_weight, key_weight, value_weight, out_weight = items
    widened = features.astype(jnp.float32)
    inverse = lax.rsqrt(lax.optimization_barrier(jnp.mean(widened * widened, axis=1, keepdims=True)) + 1e-06)
    normed = (widened * inverse * gain_row.astype(jnp.float32)[None, :]).astype(jnp.bfloat16)
    query = jnp.dot(normed, query_weight, preferred_element_type=jnp.float32).astype(jnp.bfloat16)
    key_rows = jnp.dot(memory, key_weight, preferred_element_type=jnp.float32).astype(jnp.bfloat16)
    value_rows = jnp.dot(memory, value_weight, preferred_element_type=jnp.float32).astype(jnp.bfloat16)
    query_heads = query.reshape(QTOK, HEADS, HEAD_DIM).transpose(1, 0, 2)
    key_heads = key_rows.reshape(MTOK, HEADS, HEAD_DIM).transpose(1, 0, 2)
    value_heads = value_rows.reshape(MTOK, HEADS, HEAD_DIM).transpose(1, 0, 2)

    def one_head(triple):
        query_head, key_head, value_head = triple
        scores = jnp.dot(query_head, key_head.T, preferred_element_type=jnp.float32) + mask_bias[None, :]
        weights = jnp.exp(scores)
        denominator = lax.optimization_barrier(jnp.sum(weights, axis=1, keepdims=True))
        numerator = jnp.dot(weights.astype(jnp.bfloat16), value_head, preferred_element_type=jnp.float32)
        return (numerator / denominator).astype(jnp.bfloat16)
    attended = lax.map(one_head, (query_heads, key_heads, value_heads))
    attended = attended.transpose(1, 0, 2).reshape(QTOK, HEADS * HEAD_DIM)
    return jnp.dot(attended, out_weight, preferred_element_type=jnp.float32).astype(jnp.bfloat16)

def reference(hidden, gain, w_query, w_key, w_value, w_out, memory, keep):
    mask_bias = (keep.astype(jnp.float32) - 1.0) * 30.0

    def per_section(items):
        return section_update(items, memory, mask_bias)
    updates = lax.map(per_section, (hidden, gain, w_query, w_key, w_value, w_out))
    return jnp.roll(updates, 1, axis=0)
```

```python
import functools

import jax
import jax.numpy as jnp
from jax import lax
from jax.experimental import pallas as pl
from jax.experimental.pallas import tpu as pltpu
from jax.sharding import PartitionSpec as P

HEAD_DIM = 64
SIDES = 2
CHUNKS = 2

mask_drop = 30.0
norm_eps = 1e-06

MESH = pl.DeviceIdType.MESH


def wrap(value, length):
    return lax.rem(value, length)


def kernel(
    sections,
    seqs,
    heads,
    rows_each,
    hidden_ref,
    gain_ref,
    wq_ref,
    wk_ref,
    wv_ref,
    wo_ref,
    mem_ref,
    out_ref,
    hid,
    gain,
    wq,
    wk,
    wv,
    wo,
    mem,
    raw,
    kv,
    att,
    side_send,
    side_recv,
    line_send,
    line_recv,
    load_sem,
    hid_send,
    hid_recv,
    mem_send,
    mem_recv,
    kv_send,
    kv_recv,
    side_ssem,
    side_rsem,
    line_ssem,
    line_rsem,
):
    s, q, h = lax.axis_index("section"), lax.axis_index("seq"), lax.axis_index("head")
    lines = heads // SIDES
    line, side = h // SIDES, lax.rem(h, SIDES)
    other = 1 - side
    partner = line * SIDES + other
    tokens = hid.shape[2]
    width = hid.shape[3]
    inner = wq.shape[1]
    padded = mem.shape[2]
    next_s, prev_s = wrap(s + 1, sections), wrap(s + sections - 1, sections)

    def near(k):
        return wrap(line + k, lines)

    def at(ls):
        return ls * SIDES + side

    def opposite(ls):
        return ls * SIDES + other

    loads = {}

    def load(name, index, src, dst):
        loads[name] = pltpu.make_async_copy(src, dst, load_sem.at[index])
        loads[name].start()

    load("mem", 0, mem_ref, mem.at[s, h])
    for c in range(CHUNKS):
        load(("hid", c), 1 + c, hidden_ref.at[pl.ds(c * tokens, tokens)], hid.at[c, h])
    load("wk", 1 + CHUNKS, wk_ref, wk)
    load("wv", 2 + CHUNKS, wv_ref, wv)
    load("wq", 3 + CHUNKS, wq_ref, wq)
    load("gain", 4 + CHUNKS, gain_ref, gain)
    load("wo", 5 + CHUNKS, wo_ref, wo)

    barrier = pltpu.get_barrier_semaphore()
    peers = [(s, q, at(near(k))) for k in range(1, lines)] + [(s, q, partner)]
    peers += [(wrap(s + k, sections), q, h) for k in range(1, sections)]
    peers += [(s, wrap(q + k, seqs), h) for k in range(1, seqs)]
    peers += [(next_s, q, at(near(k))) for k in range(1, lines)]
    if sections > 2:
        peers += [(prev_s, q, at(near(k))) for k in range(1, lines)]
    for peer in peers:
        pl.semaphore_signal(barrier, inc=1, device_id=peer, device_id_type=MESH)
    pl.semaphore_wait(barrier, len(peers))

    sent = []

    def send(src, dst, ssem, rsem, device):
        copy = pltpu.make_async_remote_copy(
            src_ref=src, dst_ref=dst, send_sem=ssem, recv_sem=rsem,
            device_id=device, device_id_type=MESH,
        )
        copy.start()
        sent.append(copy)

    def arrived(dst, ssem, rsem):
        pltpu.make_async_remote_copy(
            src_ref=dst, dst_ref=dst, send_sem=ssem, recv_sem=rsem,
            device_id=(s, q, partner), device_id_type=MESH,
        ).wait_recv()

    def mem_out(block, slot, device, index):
        send(block, mem.at[s, slot], mem_send.at[index], mem_recv.at[s, slot], device)

    def mem_across(block, slot, j):
        base = lines - 1 + lines
        for k in range(1, sections):
            mem_out(block, slot, (wrap(s + k, sections), q, h), base + j * (sections - 1) + k - 1)

    def hid_lines(c):
        rows = hidden_ref.at[pl.ds(c * tokens, tokens)]
        for k in range(1, lines):
            send(rows, hid.at[c, h], hid_send.at[c, k - 1], hid_recv.at[c, h], (s, q, at(near(k))))
        send(rows, hid.at[c, h], hid_send.at[c, lines - 1], hid_recv.at[c, h], (s, q, partner))

    def hid_forward(c):
        for k in range(1, lines):
            slot = at(near(lines - k))
            arrived(hid.at[c, slot], hid_send.at[c, 0], hid_recv.at[c, slot])
            send(hid.at[c, slot], hid.at[c, slot], hid_send.at[c, lines - 1 + k],
                 hid_recv.at[c, slot], (s, q, partner))

    for k in range(1, lines):
        mem_out(mem_ref, h, (s, q, at(near(k))), k - 1)
    mem_out(mem_ref, h, (s, q, partner), lines - 1)
    mem_across(mem_ref, h, 0)
    hid_lines(0)
    for k in range(1, lines):
        slot = at(near(lines - k))
        arrived(mem.at[s, slot], mem_send.at[0], mem_recv.at[s, slot])
        mem_out(mem.at[s, slot], slot, (s, q, partner), lines - 1 + k)
        mem_across(mem.at[s, slot], slot, k)
    hid_forward(0)
    for c in range(1, CHUNKS):
        hid_lines(c)
    for k in range(lines):
        slot = opposite(near(lines - k))
        arrived(mem.at[s, slot], mem_send.at[0], mem_recv.at[s, slot])
        mem_across(mem.at[s, slot], slot, lines + k)

    loads["mem"].wait()
    loads["wk"].wait()
    loads["wv"].wait()
    block_rows = heads * padded

    def project(sj):
        rows = mem[sj].reshape(block_rows, mem.shape[3])
        into = pl.ds(pl.multiple_of(sj * block_rows, block_rows), block_rows)
        raw[into, :inner] = jnp.dot(rows, wk[...], preferred_element_type=jnp.float32).astype(jnp.bfloat16)
        raw[into, inner : 2 * inner] = jnp.dot(
            rows, wv[...], preferred_element_type=jnp.float32
        ).astype(jnp.bfloat16)
        raw[into, 2 * inner :] = rows[:, :128]

    project(s)
    for k in range(1, sections):
        sj = wrap(s + k, sections)
        for hj in range(heads):
            arrived(mem.at[sj, hj], mem_send.at[0], mem_recv.at[sj, hj])
        project(sj)
    shard = sections * heads * rows_each
    total_raw = sections * block_rows
    row = lax.broadcasted_iota(jnp.int32, (shard, total_raw), 0)
    col = lax.broadcasted_iota(jnp.int32, (shard, total_raw), 1)
    owner, place = row // rows_each, row % rows_each
    pick = (col == owner * padded + place).astype(jnp.bfloat16)
    pick_flags = (col == owner * padded + rows_each).astype(jnp.bfloat16)
    mine = pl.ds(pl.multiple_of(q * shard, shard), shard)
    kv[mine, : 2 * inner] = jnp.dot(
        pick, raw[:, : 2 * inner], preferred_element_type=jnp.float32
    ).astype(jnp.bfloat16)
    flags = jnp.dot(pick_flags, raw[:, 2 * inner :], preferred_element_type=jnp.float32)
    lane = lax.broadcasted_iota(jnp.int32, (shard, 128), 1)
    own_place = lax.broadcasted_iota(jnp.int32, (shard, 128), 0) % rows_each
    kv[mine, 2 * inner :] = jnp.where(lane == own_place, flags, 0.0).astype(jnp.bfloat16)
    for k in range(1, seqs):
        send(kv.at[mine], kv.at[mine], kv_send.at[k - 1], kv_recv.at[q], (s, wrap(q + k, seqs), h))

    head_of = lax.broadcasted_iota(jnp.int32, (tokens, inner), 1) // HEAD_DIM

    def query_of(c):
        total = jnp.zeros((tokens, inner), jnp.float32)
        squares = jnp.zeros((tokens, 1), jnp.float32)
        order = [h] + [at(near(lines - k)) for k in range(1, lines)]
        order += [opposite(near(lines - k)) for k in range(lines)]
        for j, slot in enumerate(order):
            if j == 0:
                loads[("hid", c)].wait()
            elif j >= lines:
                arrived(hid.at[c, slot], hid_send.at[c, 0], hid_recv.at[c, slot])
            span = pl.ds(pl.multiple_of(slot * width, width), width)
            x = hid[c, slot].astype(jnp.float32)
            squares += jnp.sum(x * x, axis=1, keepdims=True)
            scaled = (x * gain[:, span].astype(jnp.float32)).astype(jnp.bfloat16)
            total += jnp.dot(scaled, wq[span, :], preferred_element_type=jnp.float32)
        inverse = lax.rsqrt(squares / (heads * width) + norm_eps)
        return (total * inverse).astype(jnp.bfloat16)

    def attend(c, query):
        ones = jnp.ones((8, 128), jnp.bfloat16)
        kept = lax.dot_general(
            ones, kv[:, 2 * inner :], (((1,), (1,)), ((), ())), preferred_element_type=jnp.float32
        )
        bias = (kept[:1] - 1.0) * mask_drop
        attended = jnp.zeros((tokens, inner), jnp.float32)
        for head in range(inner // HEAD_DIM):
            only = jnp.where(head_of == head, query, jnp.zeros_like(query))
            scores = lax.dot_general(
                only, kv[:, :inner], (((1,), (1,)), ((), ())), preferred_element_type=jnp.float32
            )
            weights = jnp.exp(scores + bias)
            denominator = jnp.sum(weights, axis=1, keepdims=True)
            numerator = jnp.dot(
                weights.astype(jnp.bfloat16), kv[:, inner : 2 * inner], preferred_element_type=jnp.float32
            )
            attended = jnp.where(head_of == head, numerator / denominator, attended)
        att[c] = attended.astype(jnp.bfloat16)

    def term(c, slot):
        span = pl.ds(pl.multiple_of(slot * width, width), width)
        return jnp.dot(att[c], wo[:, span], preferred_element_type=jnp.float32)

    def to_side(c):
        for k in range(lines):
            to = near(1 + k)
            side_send[c, k] = term(c, opposite(to)).astype(jnp.bfloat16)
            send(side_send.at[c, k], side_recv.at[c, to], side_ssem.at[c, k], side_rsem.at[c, to],
                 (s, q, partner))

    def to_lines(c):
        for k in range(lines):
            to = near(1 + k)
            own = term(c, at(to))
            arrived(side_recv.at[c, to], side_ssem.at[c, 0], side_rsem.at[c, to])
            line_send[c, k] = (own + side_recv[c, to].astype(jnp.float32)).astype(jnp.bfloat16)
            send(line_send.at[c, k], line_recv.at[c, line], line_ssem.at[c, k],
                 line_rsem.at[c, line], (next_s, q, at(to)))

    for c in range(CHUNKS):
        if c == 0:
            loads["wq"].wait()
            loads["gain"].wait()
        if c + 1 < CHUNKS:
            hid_forward(c + 1)
        query = query_of(c)
        if c == 0:
            for k in range(1, seqs):
                qj = wrap(q + k, seqs)
                theirs = kv.at[pl.ds(pl.multiple_of(qj * shard, shard), shard)]
                arrived(theirs, kv_send.at[0], kv_recv.at[qj])
        attend(c, query)
        if c == 0:
            loads["wo"].wait()
        to_side(c)
        if c >= 1:
            to_lines(c - 1)
    to_lines(CHUNKS - 1)
    for c in range(CHUNKS):
        update = jnp.zeros((tokens, width), jnp.float32)
        for ls in range(lines):
            arrived(line_recv.at[c, ls], line_ssem.at[c, 0], line_rsem.at[c, ls])
            update += line_recv[c, ls].astype(jnp.float32)
        out_ref[c * tokens : (c + 1) * tokens, :] = update.astype(jnp.bfloat16)
    for copy in sent:
        copy.wait_send()


def shards(sizes, hidden, gain, w_query, w_key, w_value, w_out, memory, keep):
    sections, seqs, heads = sizes
    lines = heads // SIDES
    all_tokens, width = hidden.shape[1:]
    tokens = all_tokens // CHUNKS
    rows_each, model = memory.shape
    padded = (rows_each + 1 + 15) // 16 * 16
    inner = w_query.shape[2]
    flags = jnp.pad(keep.astype(jnp.bfloat16)[None, :], ((0, 0), (0, model - rows_each)))
    block = jnp.concatenate(
        [memory, flags, jnp.zeros((padded - rows_each - 1, model), jnp.bfloat16)], axis=0
    )
    shard = sections * heads * rows_each
    low = jnp.bfloat16
    hbm = pl.BlockSpec(memory_space=pl.ANY)
    dma = pltpu.SemaphoreType.DMA
    return pl.pallas_call(
        functools.partial(kernel, sections, seqs, heads, rows_each),
        out_shape=jax.ShapeDtypeStruct((all_tokens, width), low),
        in_specs=[hbm] * 7,
        out_specs=pl.BlockSpec(memory_space=pltpu.VMEM),
        scratch_shapes=[
            pltpu.VMEM((CHUNKS, heads, tokens, width), low),
            pltpu.VMEM((1, model), low),
            pltpu.VMEM((model, inner), low),
            pltpu.VMEM((model, inner), low),
            pltpu.VMEM((model, inner), low),
            pltpu.VMEM((inner, model), low),
            pltpu.VMEM((sections, heads, padded, model), low),
            pltpu.VMEM((sections * heads * padded, 2 * inner + 128), low),
            pltpu.VMEM((seqs * shard, 2 * inner + 128), low),
            pltpu.VMEM((CHUNKS, tokens, inner), low),
            pltpu.VMEM((CHUNKS, lines, tokens, width), low),
            pltpu.VMEM((CHUNKS, lines, tokens, width), low),
            pltpu.VMEM((CHUNKS, lines, tokens, width), low),
            pltpu.VMEM((CHUNKS, lines, tokens, width), low),
            dma((6 + CHUNKS,)),
            dma((CHUNKS, 2 * lines - 1)),
            dma((CHUNKS, heads)),
            dma((2 * lines - 1 + heads * (sections - 1),)),
            dma((sections, heads)),
            dma((seqs,)),
            dma((seqs,)),
            dma((CHUNKS, lines)),
            dma((CHUNKS, lines)),
            dma((CHUNKS, lines)),
            dma((CHUNKS, lines)),
        ],
        compiler_params=pltpu.CompilerParams(
            collective_id=0, has_side_effects=True, vmem_limit_bytes=48 * 1024 * 1024
        ),
    )(hidden[0], gain, w_query[0], w_key[0], w_value[0], w_out[0], block)[None]


def solution(mesh):
    in_specs = (
        P("section", "seq", "head"),
        P("section", None),
        P("section", None, "head"),
        P("section", None, "head"),
        P("section", None, "head"),
        P("section", "head", None),
        P(("section", "seq", "head"), None),
        P(("section", "seq", "head")),
    )
    out_specs = P("section", "seq", "head")
    sizes = tuple(mesh.shape[name] for name in ("section", "seq", "head"))
    return jax.shard_map(
        functools.partial(shards, sizes),
        mesh=mesh, in_specs=in_specs, out_specs=out_specs, check_vma=False,
    )
```

```python
import functools

import jax
import jax.numpy as jnp
from jax import lax
from jax.experimental import pallas as pl
from jax.experimental.pallas import tpu as pltpu
from jax.sharding import PartitionSpec as P

HEAD_DIM = 64
SIDES = 2
CHUNKS = 4

mask_drop = 30.0
norm_eps = 1e-06

MESH = pl.DeviceIdType.MESH


def wrap(value, length):
    return lax.rem(value, length)


def kernel(
    sections,
    seqs,
    heads,
    rows_each,
    hidden_ref,
    gain_ref,
    wq_ref,
    wk_ref,
    wv_ref,
    wo_ref,
    mem_ref,
    out_ref,
    hid,
    gain,
    wq,
    wk,
    wv,
    wo,
    mem,
    raw,
    kv,
    att,
    keys_t,
    bias,
    side_send,
    side_recv,
    line_send,
    line_recv,
    load_sem,
    hid_send,
    hid_recv,
    mem_send,
    mem_recv,
    kv_send,
    kv_recv,
    side_ssem,
    side_rsem,
    line_ssem,
    line_rsem,
):
    s, q, h = lax.axis_index("section"), lax.axis_index("seq"), lax.axis_index("head")
    lines = heads // SIDES
    line, side = h // SIDES, lax.rem(h, SIDES)
    other = 1 - side
    partner = line * SIDES + other
    tokens = hid.shape[2]
    width = hid.shape[3]
    inner = wq.shape[1]
    padded = mem.shape[2]
    next_s, prev_s = wrap(s + 1, sections), wrap(s + sections - 1, sections)

    def near(k):
        return wrap(line + k, lines)

    def at(ls):
        return ls * SIDES + side

    def opposite(ls):
        return ls * SIDES + other

    loads = {}

    def load(name, index, src, dst):
        loads[name] = pltpu.make_async_copy(src, dst, load_sem.at[index])
        loads[name].start()

    load("mem", 0, mem_ref, mem.at[s, h])
    for c in range(CHUNKS):
        load(("hid", c), 1 + c, hidden_ref.at[pl.ds(c * tokens, tokens)], hid.at[c, h])
    barrier = pltpu.get_barrier_semaphore()
    peers = [(s, q, at(near(k))) for k in range(1, lines)] + [(s, q, partner)]
    peers += [(wrap(s + k, sections), q, h) for k in range(1, sections)]
    peers += [(s, wrap(q + k, seqs), h) for k in range(1, seqs)]
    peers += [(next_s, q, at(near(k))) for k in range(1, lines)]
    if sections > 2:
        peers += [(prev_s, q, at(near(k))) for k in range(1, lines)]
    for peer in peers:
        pl.semaphore_signal(barrier, inc=1, device_id=peer, device_id_type=MESH)
    pl.semaphore_wait(barrier, len(peers))

    sent = []

    def send(src, dst, ssem, rsem, device):
        copy = pltpu.make_async_remote_copy(
            src_ref=src, dst_ref=dst, send_sem=ssem, recv_sem=rsem,
            device_id=device, device_id_type=MESH,
        )
        copy.start()
        sent.append(copy)

    def arrived(dst, ssem, rsem):
        pltpu.make_async_remote_copy(
            src_ref=dst, dst_ref=dst, send_sem=ssem, recv_sem=rsem,
            device_id=(s, q, partner), device_id_type=MESH,
        ).wait_recv()

    def mem_out(block, slot, device, index):
        send(block, mem.at[s, slot], mem_send.at[index], mem_recv.at[s, slot], device)

    def mem_across(block, slot, j):
        base = lines - 1 + lines
        for k in range(1, sections):
            mem_out(block, slot, (wrap(s + k, sections), q, h), base + j * (sections - 1) + k - 1)

    def hid_lines(c):
        rows = hidden_ref.at[pl.ds(c * tokens, tokens)]
        for k in range(1, lines):
            send(rows, hid.at[c, h], hid_send.at[c, k - 1], hid_recv.at[c, h], (s, q, at(near(k))))
        send(rows, hid.at[c, h], hid_send.at[c, lines - 1], hid_recv.at[c, h], (s, q, partner))

    def hid_forward(c):
        for k in range(1, lines):
            slot = at(near(lines - k))
            arrived(hid.at[c, slot], hid_send.at[c, 0], hid_recv.at[c, slot])
            send(hid.at[c, slot], hid.at[c, slot], hid_send.at[c, lines - 1 + k],
                 hid_recv.at[c, slot], (s, q, partner))

    for k in range(1, lines):
        mem_out(mem_ref, h, (s, q, at(near(k))), k - 1)
    mem_out(mem_ref, h, (s, q, partner), lines - 1)
    mem_across(mem_ref, h, 0)
    hid_lines(0)
    load("wk", 1 + CHUNKS, wk_ref, wk)
    load("wv", 2 + CHUNKS, wv_ref, wv)
    load("wq", 3 + CHUNKS, wq_ref, wq)
    load("gain", 4 + CHUNKS, gain_ref, gain)
    load("wo", 5 + CHUNKS, wo_ref, wo)
    for k in range(1, lines):
        slot = at(near(lines - k))
        arrived(mem.at[s, slot], mem_send.at[0], mem_recv.at[s, slot])
        mem_out(mem.at[s, slot], slot, (s, q, partner), lines - 1 + k)
        mem_across(mem.at[s, slot], slot, k)
    hid_forward(0)
    for c in range(1, CHUNKS):
        hid_lines(c)
    for k in range(lines):
        slot = opposite(near(lines - k))
        arrived(mem.at[s, slot], mem_send.at[0], mem_recv.at[s, slot])
        mem_across(mem.at[s, slot], slot, lines + k)

    loads["mem"].wait()
    loads["wk"].wait()
    loads["wv"].wait()
    block_rows = heads * padded

    def project(sj):
        rows = mem[sj].reshape(block_rows, mem.shape[3])
        into = pl.ds(pl.multiple_of(sj * block_rows, block_rows), block_rows)
        raw[into, :inner] = jnp.dot(rows, wk[...], preferred_element_type=jnp.float32).astype(jnp.bfloat16)
        raw[into, inner : 2 * inner] = jnp.dot(
            rows, wv[...], preferred_element_type=jnp.float32
        ).astype(jnp.bfloat16)
        raw[into, 2 * inner :] = rows[:, :128]

    project(s)
    for k in range(1, sections):
        sj = wrap(s + k, sections)
        for hj in range(heads):
            arrived(mem.at[sj, hj], mem_send.at[0], mem_recv.at[sj, hj])
        project(sj)
    shard = sections * heads * rows_each
    total_raw = sections * block_rows
    row = lax.broadcasted_iota(jnp.int32, (shard, total_raw), 0)
    col = lax.broadcasted_iota(jnp.int32, (shard, total_raw), 1)
    shift = padded.bit_length() - 1
    owner, place = lax.shift_right_logical(col, shift), col & (padded - 1)
    start = owner * rows_each
    pick = ((row == start + place) & (place < rows_each)).astype(jnp.bfloat16)
    pick_flags = ((row >= start) & (row < start + rows_each) & (place == rows_each)).astype(jnp.bfloat16)
    mine = pl.ds(pl.multiple_of(q * shard, shard), shard)
    kv[mine, : 2 * inner] = jnp.dot(
        pick, raw[:, : 2 * inner], preferred_element_type=jnp.float32
    ).astype(jnp.bfloat16)
    flags = jnp.dot(pick_flags, raw[:, 2 * inner :], preferred_element_type=jnp.float32)
    lane = lax.broadcasted_iota(jnp.int32, (shard, 128), 1)
    own_row = lax.broadcasted_iota(jnp.int32, (shard, 128), 0)
    near_lane = jnp.zeros((shard, 128), jnp.bool_)
    for j in range(sections * heads):
        near_lane |= own_row == lane + j * rows_each
    kv[mine, 2 * inner :] = jnp.where(near_lane & (lane < rows_each), flags, 0.0).astype(jnp.bfloat16)
    for k in range(1, seqs):
        send(kv.at[mine], kv.at[mine], kv_send.at[k - 1], kv_recv.at[q], (s, wrap(q + k, seqs), h))

    head_of = lax.broadcasted_iota(jnp.int32, (tokens, inner), 1) // HEAD_DIM
    own_heads = inner // HEAD_DIM

    def query_of(c):
        total = jnp.zeros((tokens, inner), jnp.float32)
        squares = jnp.zeros((tokens, 1), jnp.float32)
        order = [h] + [at(near(lines - k)) for k in range(1, lines)]
        order += [opposite(near(lines - k)) for k in range(lines)]
        for j, slot in enumerate(order):
            if j == 0:
                loads[("hid", c)].wait()
            elif j >= lines:
                arrived(hid.at[c, slot], hid_send.at[c, 0], hid_recv.at[c, slot])
            span = pl.ds(pl.multiple_of(slot * width, width), width)
            x = hid[c, slot].astype(jnp.float32)
            squares += jnp.sum(x * x, axis=1, keepdims=True)
            scaled = (x * gain[:, span].astype(jnp.float32)).astype(jnp.bfloat16)
            total += jnp.dot(scaled, wq[span, :], preferred_element_type=jnp.float32)
        inverse = lax.rsqrt(squares / (heads * width) + norm_eps)
        return (total * inverse).astype(jnp.bfloat16)

    def prepare():
        kept = lax.dot_general(
            jnp.ones((8, 128), jnp.bfloat16), kv[:, 2 * inner :], (((1,), (1,)), ((), ())),
            preferred_element_type=jnp.float32,
        )
        bias[...] = (kept - 1.0) * mask_drop
        keys_t[...] = kv[:, :inner].T

    def attend(c, query):
        none = jnp.zeros_like(query)
        stacked = jnp.concatenate([jnp.where(head_of == j, query, none) for j in range(own_heads)], axis=0)
        scores = jnp.dot(stacked, keys_t[...], preferred_element_type=jnp.float32)
        weights = jnp.exp(scores + bias[:1])
        denominator = jnp.sum(weights, axis=1, keepdims=True)
        numerator = jnp.dot(
            weights.astype(jnp.bfloat16), kv[:, inner : 2 * inner], preferred_element_type=jnp.float32
        )
        ratio = numerator / denominator
        attended = ratio[:tokens]
        for j in range(1, own_heads):
            attended = jnp.where(head_of == j, ratio[j * tokens : (j + 1) * tokens], attended)
        att[c] = attended.astype(jnp.bfloat16)

    def term(c, slot):
        span = pl.ds(pl.multiple_of(slot * width, width), width)
        return jnp.dot(att[c], wo[:, span], preferred_element_type=jnp.float32)

    def to_side(c):
        for k in range(lines):
            to = near(1 + k)
            side_send[c, k] = term(c, opposite(to)).astype(jnp.bfloat16)
            send(side_send.at[c, k], side_recv.at[c, to], side_ssem.at[c, k], side_rsem.at[c, to],
                 (s, q, partner))

    def to_lines(c):
        for k in range(lines):
            to = near(1 + k)
            own = term(c, at(to))
            arrived(side_recv.at[c, to], side_ssem.at[c, 0], side_rsem.at[c, to])
            line_send[c, k] = (own + side_recv[c, to].astype(jnp.float32)).astype(jnp.bfloat16)
            send(line_send.at[c, k], line_recv.at[c, line], line_ssem.at[c, k],
                 line_rsem.at[c, line], (next_s, q, at(to)))

    for c in range(CHUNKS):
        if c == 0:
            loads["wq"].wait()
            loads["gain"].wait()
        if c + 1 < CHUNKS:
            hid_forward(c + 1)
        query = query_of(c)
        if c == 0:
            for k in range(1, seqs):
                qj = wrap(q + k, seqs)
                theirs = kv.at[pl.ds(pl.multiple_of(qj * shard, shard), shard)]
                arrived(theirs, kv_send.at[0], kv_recv.at[qj])
        if c == 0:
            prepare()
        attend(c, query)
        if c == 0:
            loads["wo"].wait()
        to_side(c)
        if c >= 1:
            to_lines(c - 1)
    to_lines(CHUNKS - 1)
    for c in range(CHUNKS):
        update = jnp.zeros((tokens, width), jnp.float32)
        for ls in range(lines):
            arrived(line_recv.at[c, ls], line_ssem.at[c, 0], line_rsem.at[c, ls])
            update += line_recv[c, ls].astype(jnp.float32)
        out_ref[c * tokens : (c + 1) * tokens, :] = update.astype(jnp.bfloat16)
    for copy in sent:
        copy.wait_send()


def shards(sizes, hidden, gain, w_query, w_key, w_value, w_out, memory, keep):
    sections, seqs, heads = sizes
    lines = heads // SIDES
    all_tokens, width = hidden.shape[1:]
    tokens = all_tokens // CHUNKS
    rows_each, model = memory.shape
    padded = 16
    while padded < rows_each + 1:
        padded *= 2
    inner = w_query.shape[2]
    flags = jnp.pad(keep.astype(jnp.bfloat16)[None, :], ((0, 0), (0, model - rows_each)))
    block = jnp.concatenate(
        [memory, flags, jnp.zeros((padded - rows_each - 1, model), jnp.bfloat16)], axis=0
    )
    shard = sections * heads * rows_each
    low = jnp.bfloat16
    hbm = pl.BlockSpec(memory_space=pltpu.HBM)
    dma = pltpu.SemaphoreType.DMA
    return pl.pallas_call(
        functools.partial(kernel, sections, seqs, heads, rows_each),
        out_shape=jax.ShapeDtypeStruct((all_tokens, width), low),
        in_specs=[hbm] * 7,
        out_specs=pl.BlockSpec(memory_space=pltpu.VMEM),
        scratch_shapes=[
            pltpu.VMEM((CHUNKS, heads, tokens, width), low),
            pltpu.VMEM((1, model), low),
            pltpu.VMEM((model, inner), low),
            pltpu.VMEM((model, inner), low),
            pltpu.VMEM((model, inner), low),
            pltpu.VMEM((inner, model), low),
            pltpu.VMEM((sections, heads, padded, model), low),
            pltpu.VMEM((sections * heads * padded, 2 * inner + 128), low),
            pltpu.VMEM((seqs * shard, 2 * inner + 128), low),
            pltpu.VMEM((CHUNKS, tokens, inner), low),
            pltpu.VMEM((inner, seqs * shard), low),
            pltpu.VMEM((8, seqs * shard), jnp.float32),
            pltpu.VMEM((CHUNKS, lines, tokens, width), low),
            pltpu.VMEM((CHUNKS, lines, tokens, width), low),
            pltpu.VMEM((CHUNKS, lines, tokens, width), low),
            pltpu.VMEM((CHUNKS, lines, tokens, width), low),
            dma((6 + CHUNKS,)),
            dma((CHUNKS, 2 * lines - 1)),
            dma((CHUNKS, heads)),
            dma((2 * lines - 1 + heads * (sections - 1),)),
            dma((sections, heads)),
            dma((seqs,)),
            dma((seqs,)),
            dma((CHUNKS, lines)),
            dma((CHUNKS, lines)),
            dma((CHUNKS, lines)),
            dma((CHUNKS, lines)),
        ],
        compiler_params=pltpu.CompilerParams(
            collective_id=0, has_side_effects=True, vmem_limit_bytes=48 * 1024 * 1024
        ),
    )(hidden[0], gain, w_query[0], w_key[0], w_value[0], w_out[0], block)[None]


def solution(mesh):
    in_specs = (
        P("section", "seq", "head"),
        P("section", None),
        P("section", None, "head"),
        P("section", None, "head"),
        P("section", None, "head"),
        P("section", "head", None),
        P(("section", "seq", "head"), None),
        P(("section", "seq", "head")),
    )
    out_specs = P("section", "seq", "head")
    sizes = tuple(mesh.shape[name] for name in ("section", "seq", "head"))
    return jax.shard_map(
        functools.partial(shards, sizes),
        mesh=mesh, in_specs=in_specs, out_specs=out_specs, check_vma=False,
    )
```

```python
import functools

import jax
import jax.numpy as jnp
from jax import lax
from jax.experimental import pallas as pl
from jax.experimental.pallas import tpu as pltpu
from jax.sharding import PartitionSpec as P

HEAD_DIM = 64
SIDES = 2
CHUNKS = 4

mask_drop = 30.0
norm_eps = 1e-06

MESH = pl.DeviceIdType.MESH


def wrap(value, length):
    return lax.rem(value, length)


def kernel(
    sections,
    seqs,
    heads,
    rows_each,
    hidden_ref,
    gain_ref,
    wq_ref,
    wk_ref,
    wv_ref,
    wo_ref,
    mem_ref,
    out_ref,
    hid,
    gain,
    wq,
    wk,
    wv,
    wo,
    mem,
    raw,
    kv,
    att,
    keys_t,
    bias,
    side_send,
    side_recv,
    line_send,
    line_recv,
    load_sem,
    hid_send,
    hid_recv,
    mem_send,
    mem_recv,
    kv_send,
    kv_recv,
    side_ssem,
    side_rsem,
    line_ssem,
    line_rsem,
):
    s, q, h = lax.axis_index("section"), lax.axis_index("seq"), lax.axis_index("head")
    lines = heads // SIDES
    line, side = h // SIDES, lax.rem(h, SIDES)
    other = 1 - side
    partner = line * SIDES + other
    tokens = hid.shape[2]
    width = hid.shape[3]
    inner = wq.shape[1]
    padded = mem.shape[2]
    next_s, prev_s = wrap(s + 1, sections), wrap(s + sections - 1, sections)

    def near(k):
        return wrap(line + k, lines)

    def at(ls):
        return ls * SIDES + side

    def opposite(ls):
        return ls * SIDES + other

    loads = {}

    def load(name, index, src, dst):
        loads[name] = pltpu.make_async_copy(src, dst, load_sem.at[index])
        loads[name].start()

    load("mem", 0, mem_ref, mem.at[s, h])
    for c in range(CHUNKS):
        load(("hid", c), 1 + c, hidden_ref.at[pl.ds(c * tokens, tokens)], hid.at[c, h])
    barrier = pltpu.get_barrier_semaphore()
    peers = [(s, q, at(near(k))) for k in range(1, lines)] + [(s, q, partner)]
    peers += [(wrap(s + k, sections), q, h) for k in range(1, sections)]
    peers += [(s, wrap(q + k, seqs), h) for k in range(1, seqs)]
    peers += [(next_s, q, at(near(k))) for k in range(1, lines)]
    if sections > 2:
        peers += [(prev_s, q, at(near(k))) for k in range(1, lines)]
    for peer in peers:
        pl.semaphore_signal(barrier, inc=1, device_id=peer, device_id_type=MESH)
    pl.semaphore_wait(barrier, len(peers))

    sent = []

    def send(src, dst, ssem, rsem, device):
        copy = pltpu.make_async_remote_copy(
            src_ref=src, dst_ref=dst, send_sem=ssem, recv_sem=rsem,
            device_id=device, device_id_type=MESH,
        )
        copy.start()
        sent.append(copy)

    def arrived(dst, ssem, rsem):
        pltpu.make_async_remote_copy(
            src_ref=dst, dst_ref=dst, send_sem=ssem, recv_sem=rsem,
            device_id=(s, q, partner), device_id_type=MESH,
        ).wait_recv()

    def mem_out(block, slot, device, index):
        send(block, mem.at[s, slot], mem_send.at[index], mem_recv.at[s, slot], device)

    def mem_across(block, slot, j):
        base = lines - 1 + lines
        for k in range(1, sections):
            mem_out(block, slot, (wrap(s + k, sections), q, h), base + j * (sections - 1) + k - 1)

    def hid_lines(c):
        rows = hidden_ref.at[pl.ds(c * tokens, tokens)]
        for k in range(1, lines):
            send(rows, hid.at[c, h], hid_send.at[c, k - 1], hid_recv.at[c, h], (s, q, at(near(k))))
        send(rows, hid.at[c, h], hid_send.at[c, lines - 1], hid_recv.at[c, h], (s, q, partner))

    def hid_forward(c):
        for k in range(1, lines):
            slot = at(near(lines - k))
            arrived(hid.at[c, slot], hid_send.at[c, 0], hid_recv.at[c, slot])
            send(hid.at[c, slot], hid.at[c, slot], hid_send.at[c, lines - 1 + k],
                 hid_recv.at[c, slot], (s, q, partner))

    for k in range(1, lines):
        mem_out(mem_ref, h, (s, q, at(near(k))), k - 1)
    mem_out(mem_ref, h, (s, q, partner), lines - 1)
    mem_across(mem_ref, h, 0)
    hid_lines(0)
    load("wk", 1 + CHUNKS, wk_ref, wk)
    load("wv", 2 + CHUNKS, wv_ref, wv)
    load("wq", 3 + CHUNKS, wq_ref, wq)
    load("gain", 4 + CHUNKS, gain_ref, gain)
    load("wo", 5 + CHUNKS, wo_ref, wo)
    for k in range(1, lines):
        slot = at(near(lines - k))
        arrived(mem.at[s, slot], mem_send.at[0], mem_recv.at[s, slot])
        mem_out(mem.at[s, slot], slot, (s, q, partner), lines - 1 + k)
        mem_across(mem.at[s, slot], slot, k)
    hid_forward(0)
    for c in range(1, CHUNKS):
        hid_lines(c)
    for k in range(lines):
        slot = opposite(near(lines - k))
        arrived(mem.at[s, slot], mem_send.at[0], mem_recv.at[s, slot])
        mem_across(mem.at[s, slot], slot, lines + k)

    for c in range(1, min(CHUNKS, 2)):
        hid_forward(c)

    loads["mem"].wait()
    loads["wk"].wait()
    loads["wv"].wait()
    block_rows = heads * padded

    def project(sj):
        rows = mem[sj].reshape(block_rows, mem.shape[3])
        into = pl.ds(pl.multiple_of(sj * block_rows, block_rows), block_rows)
        raw[into, :inner] = jnp.dot(rows, wk[...], preferred_element_type=jnp.float32).astype(jnp.bfloat16)
        raw[into, inner : 2 * inner] = jnp.dot(
            rows, wv[...], preferred_element_type=jnp.float32
        ).astype(jnp.bfloat16)
        raw[into, 2 * inner :] = rows[:, :128]

    project(s)
    for k in range(1, sections):
        sj = wrap(s + k, sections)
        for hj in range(heads):
            arrived(mem.at[sj, hj], mem_send.at[0], mem_recv.at[sj, hj])
        project(sj)
    shard = sections * heads * rows_each
    total_raw = sections * block_rows
    row = lax.broadcasted_iota(jnp.int32, (shard, total_raw), 0)
    col = lax.broadcasted_iota(jnp.int32, (shard, total_raw), 1)
    shift = padded.bit_length() - 1
    owner, place = lax.shift_right_logical(col, shift), col & (padded - 1)
    start = owner * rows_each
    pick = ((row == start + place) & (place < rows_each)).astype(jnp.bfloat16)
    pick_flags = ((row >= start) & (row < start + rows_each) & (place == rows_each)).astype(jnp.bfloat16)
    mine = pl.ds(pl.multiple_of(q * shard, shard), shard)
    kv[mine, : 2 * inner] = jnp.dot(
        pick, raw[:, : 2 * inner], preferred_element_type=jnp.float32
    ).astype(jnp.bfloat16)
    flags = jnp.dot(pick_flags, raw[:, 2 * inner :], preferred_element_type=jnp.float32)
    lane = lax.broadcasted_iota(jnp.int32, (shard, 128), 1)
    own_row = lax.broadcasted_iota(jnp.int32, (shard, 128), 0)
    near_lane = jnp.zeros((shard, 128), jnp.bool_)
    for j in range(sections * heads):
        near_lane |= own_row == lane + j * rows_each
    kv[mine, 2 * inner :] = jnp.where(near_lane & (lane < rows_each), flags, 0.0).astype(jnp.bfloat16)
    for k in range(1, seqs):
        send(kv.at[mine], kv.at[mine], kv_send.at[k - 1], kv_recv.at[q], (s, wrap(q + k, seqs), h))

    head_of = lax.broadcasted_iota(jnp.int32, (tokens, inner), 1) // HEAD_DIM
    own_heads = inner // HEAD_DIM

    def query_of(c):
        total = jnp.zeros((tokens, inner), jnp.float32)
        squares = jnp.zeros((tokens, 1), jnp.float32)
        order = [h] + [at(near(lines - k)) for k in range(1, lines)]
        order += [opposite(near(lines - k)) for k in range(lines)]
        for j, slot in enumerate(order):
            if j == 0:
                loads[("hid", c)].wait()
            elif j >= lines:
                arrived(hid.at[c, slot], hid_send.at[c, 0], hid_recv.at[c, slot])
            span = pl.ds(pl.multiple_of(slot * width, width), width)
            x = hid[c, slot].astype(jnp.float32)
            squares += jnp.sum(x * x, axis=1, keepdims=True)
            scaled = (x * gain[:, span].astype(jnp.float32)).astype(jnp.bfloat16)
            total += jnp.dot(scaled, wq[span, :], preferred_element_type=jnp.float32)
        inverse = lax.rsqrt(squares / (heads * width) + norm_eps)
        return (total * inverse).astype(jnp.bfloat16)

    def prepare():
        kept = lax.dot_general(
            jnp.ones((8, 128), jnp.bfloat16), kv[:, 2 * inner :], (((1,), (1,)), ((), ())),
            preferred_element_type=jnp.float32,
        )
        bias[...] = (kept - 1.0) * mask_drop
        keys_t[...] = kv[:, :inner].T

    def attend(c, query):
        none = jnp.zeros_like(query)
        stacked = jnp.concatenate([jnp.where(head_of == j, query, none) for j in range(own_heads)], axis=0)
        scores = jnp.dot(stacked, keys_t[...], preferred_element_type=jnp.float32)
        weights = jnp.exp(scores + bias[:1])
        denominator = jnp.sum(weights, axis=1, keepdims=True)
        numerator = jnp.dot(
            weights.astype(jnp.bfloat16), kv[:, inner : 2 * inner], preferred_element_type=jnp.float32
        )
        ratio = numerator / denominator
        attended = ratio[:tokens]
        for j in range(1, own_heads):
            attended = jnp.where(head_of == j, ratio[j * tokens : (j + 1) * tokens], attended)
        att[c] = attended.astype(jnp.bfloat16)

    def term(c, slot):
        span = pl.ds(pl.multiple_of(slot * width, width), width)
        return jnp.dot(att[c], wo[:, span], preferred_element_type=jnp.float32)

    def to_side(c):
        for k in range(lines):
            to = near(1 + k)
            side_send[c, k] = term(c, opposite(to)).astype(jnp.bfloat16)
            send(side_send.at[c, k], side_recv.at[c, to], side_ssem.at[c, k], side_rsem.at[c, to],
                 (s, q, partner))

    def to_lines(c):
        for k in range(lines):
            to = near(1 + k)
            own = term(c, at(to))
            arrived(side_recv.at[c, to], side_ssem.at[c, 0], side_rsem.at[c, to])
            line_send[c, k] = (own + side_recv[c, to].astype(jnp.float32)).astype(jnp.bfloat16)
            send(line_send.at[c, k], line_recv.at[c, line], line_ssem.at[c, k],
                 line_rsem.at[c, line], (next_s, q, at(to)))

    for c in range(CHUNKS):
        if c == 0:
            loads["wq"].wait()
            loads["gain"].wait()
        if c + 2 < CHUNKS:
            hid_forward(c + 2)
        query = query_of(c)
        if c == 0:
            for k in range(1, seqs):
                qj = wrap(q + k, seqs)
                theirs = kv.at[pl.ds(pl.multiple_of(qj * shard, shard), shard)]
                arrived(theirs, kv_send.at[0], kv_recv.at[qj])
        if c == 0:
            prepare()
        attend(c, query)
        if c == 0:
            loads["wo"].wait()
        to_side(c)
        if c >= 1:
            to_lines(c - 1)
    to_lines(CHUNKS - 1)
    for c in range(CHUNKS):
        update = jnp.zeros((tokens, width), jnp.float32)
        for ls in range(lines):
            arrived(line_recv.at[c, ls], line_ssem.at[c, 0], line_rsem.at[c, ls])
            update += line_recv[c, ls].astype(jnp.float32)
        out_ref[c * tokens : (c + 1) * tokens, :] = update.astype(jnp.bfloat16)
    for copy in sent:
        copy.wait_send()


def shards(sizes, hidden, gain, w_query, w_key, w_value, w_out, memory, keep):
    sections, seqs, heads = sizes
    lines = heads // SIDES
    all_tokens, width = hidden.shape[1:]
    tokens = all_tokens // CHUNKS
    rows_each, model = memory.shape
    padded = 16
    while padded < rows_each + 1:
        padded *= 2
    inner = w_query.shape[2]
    flags = jnp.pad(keep.astype(jnp.bfloat16)[None, :], ((0, 0), (0, model - rows_each)))
    block = jnp.concatenate(
        [memory, flags, jnp.zeros((padded - rows_each - 1, model), jnp.bfloat16)], axis=0
    )
    shard = sections * heads * rows_each
    low = jnp.bfloat16
    hbm = pl.BlockSpec(memory_space=pltpu.HBM)
    dma = pltpu.SemaphoreType.DMA
    return pl.pallas_call(
        functools.partial(kernel, sections, seqs, heads, rows_each),
        out_shape=jax.ShapeDtypeStruct((all_tokens, width), low),
        in_specs=[hbm] * 7,
        out_specs=pl.BlockSpec(memory_space=pltpu.VMEM),
        scratch_shapes=[
            pltpu.VMEM((CHUNKS, heads, tokens, width), low),
            pltpu.VMEM((1, model), low),
            pltpu.VMEM((model, inner), low),
            pltpu.VMEM((model, inner), low),
            pltpu.VMEM((model, inner), low),
            pltpu.VMEM((inner, model), low),
            pltpu.VMEM((sections, heads, padded, model), low),
            pltpu.VMEM((sections * heads * padded, 2 * inner + 128), low),
            pltpu.VMEM((seqs * shard, 2 * inner + 128), low),
            pltpu.VMEM((CHUNKS, tokens, inner), low),
            pltpu.VMEM((inner, seqs * shard), low),
            pltpu.VMEM((8, seqs * shard), jnp.float32),
            pltpu.VMEM((CHUNKS, lines, tokens, width), low),
            pltpu.VMEM((CHUNKS, lines, tokens, width), low),
            pltpu.VMEM((CHUNKS, lines, tokens, width), low),
            pltpu.VMEM((CHUNKS, lines, tokens, width), low),
            dma((6 + CHUNKS,)),
            dma((CHUNKS, 2 * lines - 1)),
            dma((CHUNKS, heads)),
            dma((2 * lines - 1 + heads * (sections - 1),)),
            dma((sections, heads)),
            dma((seqs,)),
            dma((seqs,)),
            dma((CHUNKS, lines)),
            dma((CHUNKS, lines)),
            dma((CHUNKS, lines)),
            dma((CHUNKS, lines)),
        ],
        compiler_params=pltpu.CompilerParams(
            collective_id=0, has_side_effects=True, vmem_limit_bytes=48 * 1024 * 1024
        ),
    )(hidden[0], gain, w_query[0], w_key[0], w_value[0], w_out[0], block)[None]


def solution(mesh):
    in_specs = (
        P("section", "seq", "head"),
        P("section", None),
        P("section", None, "head"),
        P("section", None, "head"),
        P("section", None, "head"),
        P("section", "head", None),
        P(("section", "seq", "head"), None),
        P(("section", "seq", "head")),
    )
    out_specs = P("section", "seq", "head")
    sizes = tuple(mesh.shape[name] for name in ("section", "seq", "head"))
    return jax.shard_map(
        functools.partial(shards, sizes),
        mesh=mesh, in_specs=in_specs, out_specs=out_specs, check_vma=False,
    )
```
